32 devices in a mesh: group: 8 (over z, x), tensor: 4 (over y, core).
Axes of the slice: x: 2, y: 2, z: 4, core: 2. Of those that a mesh axis runs over, the one named last changes fastest.
Arguments:
- student_in: bfloat16 [1536, 1280], P('group'), may hold values from -6 to 6
- teacher_feat: bfloat16 [1536, 1536], P('group', 'tensor'), may hold values from -6 to 6
- owner: int32 [1536], replicated, may hold values from 0 to 7, as said below
- slot_row: int32 [1536], replicated, may hold values from 0 to 191, as said below
- w_up: bfloat16 [1280, 5120], P(None, 'tensor'), may hold values from -0.15625 to 0.15625
- b_up: float32 [5120], P('tensor'), may hold values from -4 to 4
- w_down: bfloat16 [5120, 1280], P('tensor'), may hold values from -0.078125 to 0.078125
- w_adapt: bfloat16 [1280, 1536], P(None, 'tensor'), may hold values from -0.15625 to 0.15625
Outputs:
- grad_adapt: float32 [1280, 1536], P(None, 'tensor')
- input_grad: bfloat16 [1536, 1280], P('group')
The draws below stay inside these ranges and needn't reach their ends.
Inputs may be any that keep to these rules, and one draw needn't show every extreme that they name: Every owner receives exactly 192 rows; the rows of one device name one owner at most 24 times, and some owner exactly 24 times. The pairs (owner, slot_row) of all rows are all different.
All inputs are finite; a program needn't handle non-finite values.
Results may differ from the reference program's by a relative error of at most 0.0085.
Values may be sent and summed in bfloat16 or wider, within the bound.
A program may use at most 64 MiB of HBM per device.

```python
import jax
import jax.numpy as jnp
from jax import lax

D = 1280
FF = 5120
WT = 1536
TOK_DEV = 192
RUN = 2
TOKENS = 1536
N_GROUP = 8


def route_table(key):
    run_count = TOK_DEV // RUN
    key_offset, key_rows, key_dest = jax.random.split(key, 3)
    offsets = jax.random.permutation(key_offset, N_GROUP)[jnp.arange(run_count) % N_GROUP]
    row_perm = jax.vmap(lambda sub: jax.random.permutation(sub, TOK_DEV))(jax.random.split(key_rows, N_GROUP))
    run_of = row_perm // RUN
    sources = jnp.arange(N_GROUP)[:, None]
    owners = (sources + offsets[run_of]) % N_GROUP
    dest_perm = jax.vmap(lambda sub: jax.random.permutation(sub, TOK_DEV))(jax.random.split(key_dest, N_GROUP))
    slots = dest_perm[owners, row_perm]
    return (owners.reshape(-1).astype(jnp.int32), slots.reshape(-1).astype(jnp.int32))


def draw_owner(key, part):
    table = route_table(key)
    return table[0]


def draw_slot_row(key, part):
    table = route_table(key)
    return table[1]


def block_scale(key, shape, shards, smallest, top_value):
    loudness, own = 1.0, jax.random.fold_in(key, 6)
    for position, shards_of in shards:
        heights = jnp.exp(jax.random.uniform(jax.random.fold_in(own, position), (shards_of,), jnp.float32, smallest / len(shards), top_value / len(shards)))
        loudness = loudness * jnp.repeat(heights, shape[position] // shards_of).reshape([-1 if axis == position else 1 for axis in range(len(shape))])
    return loudness


def normal_values(key, extent, deviation, bound, cuts=(), kind=jnp.bfloat16):
    result = deviation * jax.random.normal(key, extent, jnp.float32)
    if cuts:
        result = result * block_scale(key, extent, cuts, -0.22, 0.18)
    return jnp.clip(result, -bound, bound).astype(kind)


def setup_inputs(seed: int = 0) -> dict:
    streams_of = jax.random.split(jax.random.key(seed), 9)
    return {
        "student_in": normal_values(streams_of[0], (TOKENS, D), 1.0, 6.0, ((0, 8),)),
        "teacher_feat": normal_values(streams_of[1], (TOKENS, WT), 1.0, 6.0, ((0, 8), (1, 4))),
        "owner": draw_owner(jax.random.fold_in(streams_of[8], 71), 0),
        "slot_row": draw_slot_row(jax.random.fold_in(streams_of[8], 71), 0),
        "w_up": normal_values(streams_of[4], (D, FF), D ** -0.5, 0.15625, ((1, 4),)),
        "b_up": normal_values(streams_of[5], (FF,), 1.0, 4.0, ((0, 4),), jnp.float32),
        "w_down": normal_values(streams_of[6], (FF, D), FF ** -0.5, 0.078125, ((0, 4),)),
        "w_adapt": normal_values(streams_of[7], (D, WT), D ** -0.5, 0.15625, ((1, 4),)),
    }


def normalize(values):
    center = lax.optimization_barrier(jnp.mean(values, axis=-1, keepdims=True))
    spread = lax.optimization_barrier(jnp.mean(jnp.square(values - center), axis=-1, keepdims=True))
    return (values - center) * lax.rsqrt(spread + 1e-06)

def activate(values):
    return jax.nn.gelu(values, approximate=True)

def reference(student_in, teacher_feat, owner, slot_row, w_up, b_up, w_down, w_adapt):
    x_float = student_in.astype(jnp.float32)
    normed = normalize(x_float).astype(jnp.bfloat16)
    pre_act = jnp.dot(normed, w_up, preferred_element_type=jnp.float32) + b_up
    hidden = activate(pre_act).astype(jnp.bfloat16)
    branch = jnp.dot(hidden, w_down, preferred_element_type=jnp.float32)
    student_out = (x_float + branch).astype(jnp.bfloat16)
    adapted = jnp.dot(student_out, w_adapt, preferred_element_type=jnp.float32)
    dest_index = (owner * TOK_DEV + slot_row).astype(jnp.int32)
    target = jnp.zeros((TOKENS, WT), jnp.bfloat16).at[dest_index].set(teacher_feat)
    delta_adapt = (adapted - target.astype(jnp.float32)).astype(jnp.bfloat16)
    grad_adapt = jnp.dot(student_out.T, delta_adapt, preferred_element_type=jnp.float32) / jnp.sqrt(jnp.float32(TOKENS))
    grad_out = jnp.dot(delta_adapt, w_adapt.T, preferred_element_type=jnp.float32).astype(jnp.bfloat16)
    grad_hidden = jnp.dot(grad_out, w_down.T, preferred_element_type=jnp.float32)
    forward_value, gelu_back = jax.vjp(activate, pre_act)
    grad_pre = gelu_back(grad_hidden)[0].astype(jnp.bfloat16)
    grad_normed = jnp.dot(grad_pre, w_up.T, preferred_element_type=jnp.float32)
    forward_norm, norm_back = jax.vjp(normalize, x_float)
    input_grad = (grad_out.astype(jnp.float32) + norm_back(grad_normed)[0]).astype(jnp.bfloat16)
    return (grad_adapt, input_grad)
```

```python
import math

import jax
import jax.numpy as jnp
from jax import lax
from jax.experimental import pallas as pl
from jax.experimental.pallas import tpu as pltpu
from jax.sharding import PartitionSpec as P

RUN = 2
MESH = pl.DeviceIdType.MESH
F32 = jnp.float32
BF16 = jnp.bfloat16
NN = (((1,), (0,)), ((), ()))
NT = (((1,), (1,)), ((), ()))
TN = (((0,), (0,)), ((), ()))
GELU_K = math.sqrt(2.0 / math.pi)
GELU_A = 0.044715


def mm(a, b, dims=NN):
    return lax.dot_general(a, b, dims, preferred_element_type=F32)


def make_kernel(groups, tensors, tok, d, ff, fw, reduce_groups):
    ny = tensors // 2
    half = tok // 2
    cw = 256
    uw = math.gcd(ff, 256)
    nc = d // cw
    slots = RUN * ((tok // RUN + groups - 1) // groups)
    slots = 16 * ((slots + 15) // 16)
    nz = groups // 2
    blk = d // groups if reduce_groups else 8
    scale = 1.0 / math.sqrt(tok * groups)

    def kernel(
        x_ref, teach_ref, owner_ref, slot_ref, b_ref, wup_hbm, wdn_hbm, wad_hbm,
        ga_ref, ig_ref,
        wup, wdn, wad, wsem,
        normed, hidden, dgelu, full, part, send1, recv1, ybuf,
        s1_s, s1_r, y_s, y_r, ag_s, ag_r,
        outgoing, incoming, qt, t_s, t_r,
        adapted, delta, gh, gpre, gtot,
        gp, xsend, xrecv, zsend, zrecv, gfull, gx_s, gx_r, gz_s, gz_r, az_s, az_r, ax_s, ax_r,
        oscr, o_s, o_r,
    ):
        g = lax.axis_index("group")
        t = lax.axis_index("tensor")
        core = lax.rem(t, 2)
        y = lax.div(t, 2)
        mate = t + 1 - 2 * core
        own0 = pl.multiple_of(core * half, 16)
        oth0 = pl.multiple_of((1 - core) * half, 16)
        own = pl.ds(own0, half)
        oth = pl.ds(oth0, half)

        barrier = pltpu.get_barrier_semaphore()
        for k in range(1, tensors):
            pl.semaphore_signal(barrier, inc=1, device_id=(g, lax.rem(t + k, tensors)), device_id_type=MESH)
        for k in range(1, groups):
            pl.semaphore_signal(barrier, inc=1, device_id=(lax.rem(g + k, groups), t), device_id_type=MESH)

        loads = [
            pltpu.make_async_copy(src, dst, wsem.at[i])
            for i, (src, dst) in enumerate(((wup_hbm, wup), (wdn_hbm, wdn), (wad_hbm, wad)))
        ]
        for c in loads:
            c.start()

        sends = []

        def remote(src, dst, ss, rs, dev):
            c = pltpu.make_async_remote_copy(
                src_ref=src, dst_ref=dst, send_sem=ss, recv_sem=rs, device_id=dev, device_id_type=MESH
            )
            c.start()
            sends.append(c)
            return c

        xf = x_ref[...].astype(F32)
        cen = jnp.mean(xf, axis=-1, keepdims=True)
        dev_ = xf - cen
        rstd = lax.rsqrt(jnp.mean(jnp.square(dev_), axis=-1, keepdims=True) + 1e-06)
        normed[...] = (dev_ * rstd).astype(BF16)
        loads[0].wait()
        for j in range(ff // uw):
            cs = slice(j * uw, (j + 1) * uw)
            pre = mm(normed[...], wup[:, cs]) + b_ref[:, cs]
            sq = pre * pre
            th = jnp.tanh(GELU_K * pre * (1.0 + GELU_A * sq))
            hidden[:, cs] = (0.5 * pre * (1.0 + th)).astype(BF16)
            dgelu[:, cs] = 0.5 * (1.0 + th) + 0.5 * GELU_K * pre * (1.0 - th * th) * (1.0 + 3.0 * GELU_A * sq)

        pl.semaphore_wait(barrier, tensors - 1 + groups - 1)
        loads[1].wait()

        state = {}

        def stage1(a, j, value):
            part[a, j] = value
            send1[a, j] = part[a, j, oth, :].astype(BF16)
            state["s1", a, j] = remote(
                send1.at[a, j], recv1.at[a, j], s1_s.at[a, j], s1_r.at[a, j], (g, mate)
            )

        def stage2(a, j):
            state["s1", a, j].wait_recv()
            ybuf[a, j, y] = (part[a, j, own, :] + recv1[a, j].astype(F32)).astype(BF16)
            state["y", a, j] = [
                remote(
                    ybuf.at[a, j, y], ybuf.at[a, j, y], y_s.at[a, j, k - 1], y_r.at[a, j, k - 1],
                    (g, lax.rem(y + k, ny) * 2 + core),
                )
                for k in range(1, ny)
            ]

        def total(a, j):
            for c in state["y", a, j]:
                c.wait_recv()
            s = ybuf[a, j, 0].astype(F32)
            for k in range(1, ny):
                s = s + ybuf[a, j, k].astype(F32)
            return s

        def stage3(a, j, finish):
            full[a, j, own, :] = finish(total(a, j), j).astype(BF16)
            state["ag", a, j] = remote(
                full.at[a, j, own, :], full.at[a, j, own, :], ag_s.at[a, j], ag_r.at[a, j], (g, mate)
            )

        def reduce_loop(a, product):
            for j in range(nc):
                stage1(a, j, product(j))
                if j >= 1:
                    stage2(a, j - 1)
            stage2(a, nc - 1)

        def gather_loop(a, finish, consume):
            for j in range(nc):
                stage3(a, j, finish)
                if j >= 1:
                    state["ag", a, j - 1].wait_recv()
                    consume(j - 1)
            state["ag", a, nc - 1].wait_recv()
            consume(nc - 1)

        reduce_loop(0, lambda j: mm(hidden[...], wdn[:, j * cw:(j + 1) * cw]))

        ir = lax.broadcasted_iota(jnp.int32, (tok, tok), 0)
        ic = lax.broadcasted_iota(jnp.int32, (tok, tok), 1)
        own_row = owner_ref[pl.ds(g, 1), :]
        own_bc = jnp.broadcast_to(own_row, (tok, tok))
        own_col = jnp.sum(jnp.where(ir == ic, own_bc, 0).astype(F32), axis=1, keepdims=True)
        before = ir < ic
        same = jnp.where((own_col == own_bc.astype(F32)) & before, 1.0, 0.0)
        rank_row = jnp.sum(same, axis=0, keepdims=True)
        place = own_row.astype(F32) * slots + rank_row
        srow = lax.broadcasted_iota(jnp.int32, (groups * slots, tok), 0).astype(F32)
        pick = jnp.where(srow == place, 1.0, 0.0).astype(BF16)
        outgoing[...] = mm(pick, teach_ref[...]).astype(BF16).reshape(groups, slots, fw)
        teach = []
        for k in range(1, groups):
            to = lax.rem(g + k, groups)
            teach.append(
                remote(outgoing.at[to], incoming.at[g], t_s.at[k - 1], t_r.at[k - 1], (to, t))
            )
        incoming[g] = outgoing[g]
        mine = owner_ref[...] == g
        tri = jnp.where(before, 1.0, 0.0).astype(BF16)
        rank = mm(jnp.where(mine, 1.0, 0.0).astype(BF16), tri)
        rank = jnp.where(mine, rank, -1.0)
        dest1 = slot_ref[...].astype(F32) + 1.0
        krow = lax.broadcasted_iota(jnp.int32, (slots, tok), 0).astype(F32)
        lane = lax.broadcasted_iota(jnp.int32, (slots, tok), 1).astype(F32)
        for s in range(groups):
            hit = jnp.where(krow == rank[s:s + 1, :], dest1[s:s + 1, :], 0.0)
            dest = jnp.sum(hit, axis=1, keepdims=True) - 1.0
            qt[s * slots:(s + 1) * slots, :] = jnp.where(lane == dest, 1.0, 0.0).astype(BF16)

        loads[2].wait()
        adapted[...] = jnp.zeros_like(adapted)

        def add_input(s, j):
            return s + x_ref[own, j * cw:(j + 1) * cw].astype(F32)

        def adapt(j):
            adapted[...] += mm(full[0, j], wad[j * cw:(j + 1) * cw, :])

        gather_loop(0, add_input, adapt)
        for c in teach:
            c.wait_recv()
        target = mm(qt[...], incoming[...].reshape(groups * slots, fw), TN)
        delta[...] = (adapted[...] - target).astype(BF16)

        reduce_loop(1, lambda j: mm(delta[...], wad[j * cw:(j + 1) * cw, :], NT))
        for j in range(nc):
            gp[j * cw:(j + 1) * cw, :] = mm(full[0, j], delta[...], TN)

        if reduce_groups:
            gx = lax.rem(g, 2)
            gz = lax.div(g, 2)

            def rows(xx, zz):
                return pl.ds(pl.multiple_of((xx * nz + zz) * blk, 16), blk)

            xmate = (gz * 2 + 1 - gx, t)
            xcopy, zcopy, azcopy, axcopy = {}, {}, {}, {}
            for k in list(range(1, nz)) + [0]:
                zz = lax.rem(gz + k, nz)
                xsend[k] = gp[rows(1 - gx, zz), :].astype(BF16)
                xcopy[k] = remote(xsend.at[k], xrecv.at[k], gx_s.at[k], gx_r.at[k], xmate)

            def z_step(k):
                xcopy[k].wait_recv()
                zz = lax.rem(gz + k, nz)
                zsend[k - 1] = (gp[rows(gx, zz), :] + xrecv[k].astype(F32)).astype(BF16)
                zcopy[k] = remote(
                    zsend.at[k - 1], zrecv.at[k - 1], gz_s.at[k - 1], gz_r.at[k - 1], (zz * 2 + gx, t)
                )

            def z_sum():
                xcopy[0].wait_recv()
                s = gp[rows(gx, gz), :] + xrecv[0].astype(F32)
                for k in range(1, nz):
                    zcopy[k].wait_recv()
                    s = s + zrecv[k - 1].astype(F32)
                b = gx * nz + gz
                gfull[b] = (s * scale).astype(BF16)
                for k in range(1, nz):
                    zz = lax.rem(gz + k, nz)
                    azcopy[k] = remote(
                        gfull.at[b], gfull.at[b], az_s.at[k - 1], az_r.at[k - 1], (zz * 2 + gx, t)
                    )
                axcopy[0] = remote(gfull.at[b], gfull.at[b], ax_s.at[0], ax_r.at[0], xmate)

            def z_gather(k):
                azcopy[k].wait_recv()
                b = gx * nz + lax.rem(gz - k + nz, nz)
                axcopy[k] = remote(gfull.at[b], gfull.at[b], ax_s.at[k], ax_r.at[k], xmate)
        else:
            ga_ref[...] = gp[...]

        gh[...] = jnp.zeros_like(gh)

        def back(j):
            gh[...] += mm(full[1, j], wdn[:, j * cw:(j + 1) * cw], NT)

        gather_loop(1, lambda s, j: s, back)
        gpre[...] = (gh[...] * dgelu[...]).astype(BF16)
        reduce_loop(2, lambda j: mm(gpre[...], wup[j * cw:(j + 1) * cw, :], NT))
        if reduce_groups:
            for k in range(1, nz):
                z_step(k)
        for j in range(nc):
            gtot[:, j * cw:(j + 1) * cw] = total(2, j)
        gn = gtot[...]
        xo = x_ref[own, :].astype(F32)
        cen = jnp.mean(xo, axis=-1, keepdims=True)
        dv = xo - cen
        r = lax.rsqrt(jnp.mean(jnp.square(dv), axis=-1, keepdims=True) + 1e-06)
        yn = dv * r
        gmean = jnp.mean(gn, axis=-1, keepdims=True)
        gy = jnp.mean(gn * yn, axis=-1, keepdims=True)
        dx = r * (gn - gmean - yn * gy)
        for j in range(nc):
            cs = slice(j * cw, (j + 1) * cw)
            oscr[own, cs] = (full[1, j, own, :].astype(F32) + dx[:, cs]).astype(BF16)
        ocopy = remote(oscr.at[own, :], oscr.at[own, :], o_s.at[0], o_r.at[0], (g, mate))
        if reduce_groups:
            z_sum()
        ocopy.wait_recv()
        ig_ref[...] = oscr[...]
        if reduce_groups:
            for k in range(1, nz):
                z_gather(k)
            for k in range(nz):
                axcopy[k].wait_recv()
            ga_ref[...] = gfull[...].astype(F32).reshape(d, fw)
        for c in sends:
            c.wait_send()

    vm = pltpu.VMEM
    dma = pltpu.SemaphoreType.DMA
    gb = (nz, blk, fw) if reduce_groups else (1, 16, 128)
    zb = (nz - 1, blk, fw) if reduce_groups else (1, 16, 128)
    fb = (groups, blk, fw) if reduce_groups else (1, 16, 128)
    nsem = nz if reduce_groups else 1
    scratch = [
        vm((d, ff), BF16), vm((ff, d), BF16), vm((d, fw), BF16), dma((3,)),
        vm((tok, d), BF16), vm((tok, ff), BF16), vm((tok, ff), F32),
        vm((2, nc, tok, cw), BF16), vm((3, nc, tok, cw), F32),
        vm((3, nc, half, cw), BF16), vm((3, nc, half, cw), BF16), vm((3, nc, ny, half, cw), BF16),
        dma((3, nc)), dma((3, nc)), dma((3, nc, ny - 1)), dma((3, nc, ny - 1)), dma((2, nc)), dma((2, nc)),
        vm((groups, slots, fw), BF16), vm((groups, slots, fw), BF16), vm((groups * slots, tok), BF16),
        dma((groups - 1,)), dma((groups - 1,)),
        vm((tok, fw), F32), vm((tok, fw), BF16), vm((tok, ff), F32), vm((tok, ff), BF16), vm((half, d), F32),
        vm((d, fw), F32), vm(gb, BF16), vm(gb, BF16), vm(zb, BF16), vm(zb, BF16), vm(fb, BF16),
        dma((nsem,)), dma((nsem,)), dma((nsem,)), dma((nsem,)),
        dma((nsem,)), dma((nsem,)), dma((nsem,)), dma((nsem,)),
        vm((tok, d), BF16), dma((1,)), dma((1,)),
    ]
    vspec = pl.BlockSpec(memory_space=pltpu.VMEM)
    aspec = pl.BlockSpec(memory_space=pl.ANY)
    return pl.pallas_call(
        kernel,
        out_shape=(jax.ShapeDtypeStruct((d, fw), F32), jax.ShapeDtypeStruct((tok, d), BF16)),
        in_specs=[vspec] * 5 + [aspec] * 3,
        out_specs=(vspec, vspec),
        scratch_shapes=scratch,
        compiler_params=pltpu.CompilerParams(
            collective_id=0, has_side_effects=True, vmem_limit_bytes=56 * 1024 * 1024
        ),
    )


def solution(mesh):
    groups = mesh.shape["group"]
    tensors = mesh.shape["tensor"]

    def per_device(student_in, teacher_feat, owner, slot_row, w_up, b_up, w_down, w_adapt):
        tok, d = student_in.shape
        fw = teacher_feat.shape[1]
        ff = w_up.shape[1]
        reduce_groups = groups % 2 == 0 and d % (groups * 16) == 0
        call = make_kernel(groups, tensors, tok, d, ff, fw, reduce_groups)
        grad_adapt, input_grad = call(
            student_in, teacher_feat, owner.reshape(groups, tok), slot_row.reshape(groups, tok),
            b_up.reshape(1, ff), w_up, w_down, w_adapt,
        )
        if not reduce_groups:
            grad_adapt = lax.psum(grad_adapt, "group") / math.sqrt(tok * groups)
        return grad_adapt, input_grad

    return jax.shard_map(
        per_device,
        mesh=mesh,
        in_specs=(
            P("group", None),
            P("group", "tensor"),
            P(),
            P(),
            P(None, "tensor"),
            P("tensor"),
            P("tensor", None),
            P(None, "tensor"),
        ),
        out_specs=(P(None, "tensor"), P("group", None)),
        check_vma=False,
    )
```

```python
import math

import jax
import jax.numpy as jnp
from jax import lax
from jax.experimental import pallas as pl
from jax.experimental.pallas import tpu as pltpu
from jax.sharding import PartitionSpec as P

RUN = 2
MESH = pl.DeviceIdType.MESH
F32 = jnp.float32
BF16 = jnp.bfloat16
NN = (((1,), (0,)), ((), ()))
NT = (((1,), (1,)), ((), ()))
TN = (((0,), (0,)), ((), ()))
GELU_K = math.sqrt(2.0 / math.pi)
GELU_A = 0.044715


def mm(a, b, dims=NN):
    return lax.dot_general(a, b, dims, preferred_element_type=F32)


def make_kernel(groups, tensors, tok, d, ff, fw, reduce_groups):
    ny = tensors // 2
    half = tok // 2
    cw = 256
    hw = cw // 2
    uw = math.gcd(ff, 256)
    nc = d // cw
    slots = RUN * ((tok // RUN + groups - 1) // groups)
    slots = 16 * ((slots + 15) // 16)
    nz = groups // 2
    blk = d // groups if reduce_groups else 8
    scale = 1.0 / math.sqrt(tok * groups)

    def kernel(
        x_ref, teach_ref, owner_in, slot_in, b_ref, wup_hbm, wdn_hbm, wad_hbm,
        ga_ref, ig_ref,
        wup, wdn, wad, wsem,
        normed, hidden, dgelu, full, part, send1, recv1, ybuf,
        s1_s, s1_r, y_s, y_r, ag_s, ag_r,
        outgoing, incoming, qt, t_s, t_r,
        adapted, delta, gh, gpre, gtot,
        so_mate, d_mate, gsum, zsend, zrecv, gfull, so_s, so_r, d_s, d_r, gz_s, gz_r, az_s, az_r, ax_s, ax_r,
        oscr, o_s, o_r, owner_ref, slot_ref,
    ):
        g = lax.axis_index("group")
        t = lax.axis_index("tensor")
        core = lax.rem(t, 2)
        y = lax.div(t, 2)
        mate = t + 1 - 2 * core
        own0 = pl.multiple_of(core * half, 16)
        oth0 = pl.multiple_of((1 - core) * half, 16)
        own = pl.ds(own0, half)
        oth = pl.ds(oth0, half)

        barrier = pltpu.get_barrier_semaphore()
        for k in range(1, tensors):
            pl.semaphore_signal(barrier, inc=1, device_id=(g, lax.rem(t + k, tensors)), device_id_type=MESH)
        for k in range(1, groups):
            pl.semaphore_signal(barrier, inc=1, device_id=(lax.rem(g + k, groups), t), device_id_type=MESH)

        loads = [
            pltpu.make_async_copy(src, dst, wsem.at[i])
            for i, (src, dst) in enumerate(((wup_hbm, wup), (wdn_hbm, wdn), (wad_hbm, wad)))
        ]
        for c in loads:
            c.start()

        sends = []

        def remote(src, dst, ss, rs, dev):
            c = pltpu.make_async_remote_copy(
                src_ref=src, dst_ref=dst, send_sem=ss, recv_sem=rs, device_id=dev, device_id_type=MESH
            )
            c.start()
            sends.append(c)
            return c

        xf = x_ref[...].astype(F32)
        cen = jnp.mean(xf, axis=-1, keepdims=True)
        dev_ = xf - cen
        rstd = lax.rsqrt(jnp.mean(jnp.square(dev_), axis=-1, keepdims=True) + 1e-06)
        normed[...] = (dev_ * rstd).astype(BF16)
        loads[0].wait()
        for j in range(ff // uw):
            cs = slice(j * uw, (j + 1) * uw)
            pre = mm(normed[...], wup[:, cs]) + b_ref[cs][None, :]
            sq = pre * pre
            th = jnp.tanh(GELU_K * pre * (1.0 + GELU_A * sq))
            hidden[:, cs] = (0.5 * pre * (1.0 + th)).astype(BF16)
            dgelu[:, cs] = 0.5 * (1.0 + th) + 0.5 * GELU_K * pre * (1.0 - th * th) * (1.0 + 3.0 * GELU_A * sq)

        pl.semaphore_wait(barrier, tensors - 1 + groups - 1)
        loads[1].wait()

        state = {}

        def stage1(a, j, value):
            part[a, j] = value
            send1[a, j] = part[a, j, oth, :].astype(BF16)
            state["s1", a, j] = remote(
                send1.at[a, j], recv1.at[a, j], s1_s.at[a, j], s1_r.at[a, j], (g, mate)
            )

        def stage2(a, j):
            state["s1", a, j].wait_recv()
            ybuf[a, j, y] = (part[a, j, own, :] + recv1[a, j].astype(F32)).astype(BF16)
            state["y", a, j] = [
                remote(
                    ybuf.at[a, j, y], ybuf.at[a, j, y], y_s.at[a, j, k - 1], y_r.at[a, j, k - 1],
                    (g, lax.rem(y + k, ny) * 2 + core),
                )
                for k in range(1, ny)
            ]

        def total(a, j):
            for c in state["y", a, j]:
                c.wait_recv()
            s = ybuf[a, j, 0].astype(F32)
            for k in range(1, ny):
                s = s + ybuf[a, j, k].astype(F32)
            return s

        def stage3(a, j, finish):
            full[a, j, own, :] = finish(total(a, j), j).astype(BF16)
            state["ag", a, j] = remote(
                full.at[a, j, own, :], full.at[a, j, own, :], ag_s.at[a, j], ag_r.at[a, j], (g, mate)
            )

        def reduce_loop(a, product):
            for j in range(nc):
                stage1(a, j, product(j))
                if j >= 1:
                    stage2(a, j - 1)
            stage2(a, nc - 1)

        def gather_loop(a, finish, consume):
            for j in range(nc):
                stage3(a, j, finish)
                if j >= 1:
                    state["ag", a, j - 1].wait_recv()
                    consume(j - 1)
            state["ag", a, nc - 1].wait_recv()
            consume(nc - 1)

        reduce_loop(0, lambda j: mm(hidden[...], wdn[:, j * cw:(j + 1) * cw]))

        for s in range(groups):
            owner_ref[s:s + 1, :] = owner_in[s * tok:(s + 1) * tok][None, :]
            slot_ref[s:s + 1, :] = slot_in[s * tok:(s + 1) * tok][None, :]
        ir = lax.broadcasted_iota(jnp.int32, (tok, tok), 0)
        ic = lax.broadcasted_iota(jnp.int32, (tok, tok), 1)
        own_row = owner_ref[pl.ds(g, 1), :]
        own_bc = jnp.broadcast_to(own_row, (tok, tok))
        own_col = jnp.sum(jnp.where(ir == ic, own_bc, 0).astype(F32), axis=1, keepdims=True)
        before = ir < ic
        same = jnp.where((own_col == own_bc.astype(F32)) & before, 1.0, 0.0)
        rank_row = jnp.sum(same, axis=0, keepdims=True)
        place = own_row.astype(F32) * slots + rank_row
        srow = lax.broadcasted_iota(jnp.int32, (groups * slots, tok), 0).astype(F32)
        pick = jnp.where(srow == place, 1.0, 0.0).astype(BF16)
        outgoing[...] = mm(pick, teach_ref[...]).astype(BF16).reshape(groups, slots, fw)
        teach = []
        for k in range(1, groups):
            to = lax.rem(g + k, groups)
            teach.append(
                remote(outgoing.at[to], incoming.at[g], t_s.at[k - 1], t_r.at[k - 1], (to, t))
            )
        incoming[g] = outgoing[g]
        mine = owner_ref[...] == g
        tri = jnp.where(before, 1.0, 0.0).astype(BF16)
        rank = mm(jnp.where(mine, 1.0, 0.0).astype(BF16), tri)
        rank = jnp.where(mine, rank, -1.0)
        dest1 = slot_ref[...].astype(F32) + 1.0
        krow = lax.broadcasted_iota(jnp.int32, (slots, tok), 0).astype(F32)
        lane = lax.broadcasted_iota(jnp.int32, (slots, tok), 1).astype(F32)
        for s in range(groups):
            hit = jnp.where(krow == rank[s:s + 1, :], dest1[s:s + 1, :], 0.0)
            dest = jnp.sum(hit, axis=1, keepdims=True) - 1.0
            qt[s * slots:(s + 1) * slots, :] = jnp.where(lane == dest, 1.0, 0.0).astype(BF16)

        loads[2].wait()
        adapted[...] = jnp.zeros_like(adapted)

        def add_input(s, j):
            return s + x_ref[own, j * cw:(j + 1) * cw].astype(F32)

        gx = lax.rem(g, 2)
        gz = lax.div(g, 2)
        xmate = (gz * 2 + 1 - gx, t)
        lane0 = pl.ds(pl.multiple_of(gx * hw, hw), hw)
        lane1 = pl.ds(pl.multiple_of((1 - gx) * hw, hw), hw)

        def adapt(j):
            if reduce_groups:
                state["so", j] = remote(full.at[0, j, :, lane1], so_mate.at[j], so_s.at[j], so_r.at[j], xmate)
            adapted[...] += mm(full[0, j], wad[j * cw:(j + 1) * cw, :])

        gather_loop(0, add_input, adapt)
        for c in teach:
            c.wait_recv()
        target = mm(qt[...], incoming[...].reshape(groups * slots, fw), TN)
        delta[...] = (adapted[...] - target).astype(BF16)

        if reduce_groups:
            dcopy = remote(delta, d_mate, d_s.at[0], d_r.at[0], xmate)

        reduce_loop(1, lambda j: mm(delta[...], wad[j * cw:(j + 1) * cw, :], NT))

        zcopy, azcopy, axcopy = {}, {}, {}

        def rows(zz):
            return pl.ds(pl.multiple_of(zz * blk, 16), blk)

        def z_send():
            dcopy.wait_recv()
            for j in range(nc):
                state["so", j].wait_recv()
                v = mm(full[0, j, :, lane0], delta[...], TN) + mm(so_mate[j], d_mate[...], TN)
                gsum[j * hw:(j + 1) * hw, :] = v
                zsend[j * hw:(j + 1) * hw, :] = v.astype(BF16)
            for k in range(1, nz):
                zz = lax.rem(gz + k, nz)
                zcopy[k] = remote(
                    zsend.at[rows(zz), :], zrecv.at[k - 1], gz_s.at[k - 1], gz_r.at[k - 1], (zz * 2 + gx, t)
                )

        def z_sum():
            s = gsum[rows(gz), :]
            for k in range(1, nz):
                zcopy[k].wait_recv()
                s = s + zrecv[k - 1].astype(F32)
            gfull[gx, rows(gz), :] = (s * scale).astype(BF16)
            blkref = gfull.at[gx, rows(gz), :]
            for k in range(1, nz):
                zz = lax.rem(gz + k, nz)
                azcopy[k] = remote(blkref, blkref, az_s.at[k - 1], az_r.at[k - 1], (zz * 2 + gx, t))
            axcopy[0] = remote(blkref, blkref, ax_s.at[0], ax_r.at[0], xmate)

        def z_gather(k):
            azcopy[k].wait_recv()
            blkref = gfull.at[gx, rows(lax.rem(gz - k + nz, nz)), :]
            axcopy[k] = remote(blkref, blkref, ax_s.at[k], ax_r.at[k], xmate)

        if reduce_groups:
            z_send()
        else:
            for j in range(nc):
                ga_ref[j * cw:(j + 1) * cw, :] = mm(full[0, j], delta[...], TN)

        gh[...] = jnp.zeros_like(gh)

        def back(j):
            gh[...] += mm(full[1, j], wdn[:, j * cw:(j + 1) * cw], NT)

        gather_loop(1, lambda s, j: s, back)
        gpre[...] = (gh[...] * dgelu[...]).astype(BF16)
        reduce_loop(2, lambda j: mm(gpre[...], wup[j * cw:(j + 1) * cw, :], NT))
        if reduce_groups:
            z_sum()
        for j in range(nc):
            gtot[:, j * cw:(j + 1) * cw] = total(2, j)
        if reduce_groups:
            z_gather(1)
        gn = gtot[...]
        xo = x_ref[own, :].astype(F32)
        cen = jnp.mean(xo, axis=-1, keepdims=True)
        dv = xo - cen
        r = lax.rsqrt(jnp.mean(jnp.square(dv), axis=-1, keepdims=True) + 1e-06)
        yn = dv * r
        gmean = jnp.mean(gn, axis=-1, keepdims=True)
        gy = jnp.mean(gn * yn, axis=-1, keepdims=True)
        dx = r * (gn - gmean - yn * gy)
        for j in range(nc):
            cs = slice(j * cw, (j + 1) * cw)
            oscr[own, cs] = (full[1, j, own, :].astype(F32) + dx[:, cs]).astype(BF16)
        ocopy = remote(oscr.at[own, :], oscr.at[own, :], o_s.at[0], o_r.at[0], (g, mate))
        if reduce_groups:
            for k in range(2, nz):
                z_gather(k)
        ocopy.wait_recv()
        ig_ref[...] = oscr[...]
        if reduce_groups:
            for k in range(nz):
                axcopy[k].wait_recv()
            for j in range(nc):
                for xx in range(2):
                    r0 = j * cw + xx * hw
                    ga_ref[r0:r0 + hw, :] = gfull[xx, j * hw:(j + 1) * hw, :]
        for c in sends:
            c.wait_send()

    vm = pltpu.VMEM
    dma = pltpu.SemaphoreType.DMA
    gb = (d // 2, fw) if reduce_groups else (16, 128)
    zb = (nz - 1, blk, fw) if reduce_groups else (1, 16, 128)
    fb = (2, d // 2, fw) if reduce_groups else (1, 16, 128)
    mb = (nc, tok, hw) if reduce_groups else (1, 16, 128)
    db = (tok, fw) if reduce_groups else (16, 128)
    nsem = nz if reduce_groups else 1
    scratch = [
        vm((d, ff), BF16), vm((ff, d), BF16), vm((d, fw), BF16), dma((3,)),
        vm((tok, d), BF16), vm((tok, ff), BF16), vm((tok, ff), F32),
        vm((2, nc, tok, cw), BF16), vm((3, nc, tok, cw), F32),
        vm((3, nc, half, cw), BF16), vm((3, nc, half, cw), BF16), vm((3, nc, ny, half, cw), BF16),
        dma((3, nc)), dma((3, nc)), dma((3, nc, ny - 1)), dma((3, nc, ny - 1)), dma((2, nc)), dma((2, nc)),
        vm((groups, slots, fw), BF16), vm((groups, slots, fw), BF16), vm((groups * slots, tok), BF16),
        dma((groups - 1,)), dma((groups - 1,)),
        vm((tok, fw), F32), vm((tok, fw), BF16), vm((tok, ff), F32), vm((tok, ff), BF16), vm((half, d), F32),
        vm(mb, BF16), vm(db, BF16), vm(gb, F32), vm(gb, BF16), vm(zb, BF16), vm(fb, BF16),
        dma((nc,)), dma((nc,)), dma((1,)), dma((1,)), dma((nsem,)), dma((nsem,)),
        dma((nsem,)), dma((nsem,)), dma((nsem,)), dma((nsem,)),
        vm((tok, d), BF16), dma((1,)), dma((1,)), vm((groups, tok), jnp.int32), vm((groups, tok), jnp.int32),
    ]
    vspec = pl.BlockSpec(memory_space=pltpu.VMEM)
    aspec = pl.BlockSpec(memory_space=pl.ANY)
    return pl.pallas_call(
        kernel,
        out_shape=(jax.ShapeDtypeStruct((d, fw), BF16 if reduce_groups else F32), jax.ShapeDtypeStruct((tok, d), BF16)),
        in_specs=[vspec] * 5 + [aspec] * 3,
        out_specs=(vspec, vspec),
        scratch_shapes=scratch,
        compiler_params=pltpu.CompilerParams(
            collective_id=0, has_side_effects=True, vmem_limit_bytes=56 * 1024 * 1024
        ),
    )


def solution(mesh):
    groups = mesh.shape["group"]
    tensors = mesh.shape["tensor"]

    def per_device(student_in, teacher_feat, owner, slot_row, w_up, b_up, w_down, w_adapt):
        tok, d = student_in.shape
        fw = teacher_feat.shape[1]
        ff = w_up.shape[1]
        reduce_groups = groups % 2 == 0 and d % (groups * 16) == 0
        call = make_kernel(groups, tensors, tok, d, ff, fw, reduce_groups)
        grad_adapt, input_grad = call(
            student_in, teacher_feat, owner, slot_row, b_up, w_up, w_down, w_adapt,
        )
        if reduce_groups:
            grad_adapt = grad_adapt.astype(F32)
        else:
            grad_adapt = lax.psum(grad_adapt, "group") / math.sqrt(tok * groups)
        return grad_adapt, input_grad

    return jax.shard_map(
        per_device,
        mesh=mesh,
        in_specs=(
            P("group", None),
            P("group", "tensor"),
            P(),
            P(),
            P(None, "tensor"),
            P("tensor"),
            P("tensor", None),
            P(None, "tensor"),
        ),
        out_specs=(P(None, "tensor"), P("group", None)),
        check_vma=False,
    )
```

```python
import math

import jax
import jax.numpy as jnp
from jax import lax
from jax.experimental import pallas as pl
from jax.experimental.pallas import tpu as pltpu
from jax.sharding import PartitionSpec as P

RUN = 2
MESH = pl.DeviceIdType.MESH
F32 = jnp.float32
BF16 = jnp.bfloat16
NN = (((1,), (0,)), ((), ()))
NT = (((1,), (1,)), ((), ()))
TN = (((0,), (0,)), ((), ()))
GELU_K = math.sqrt(2.0 / math.pi)
GELU_A = 0.044715


def mm(a, b, dims=NN):
    return lax.dot_general(a, b, dims, preferred_element_type=F32)


def make_kernel(groups, tensors, tok, d, ff, fw, reduce_groups):
    ny = tensors // 2
    half = tok // 2
    cw = 256
    hw = cw // 2
    uw = math.gcd(ff, 256)
    nc = d // cw
    slots = RUN * ((tok // RUN + groups - 1) // groups)
    slots = 16 * ((slots + 15) // 16)
    nz = groups // 2
    nch = fw // 128 if reduce_groups else 1
    blk = d // groups if reduce_groups else 8
    scale = 1.0 / math.sqrt(tok * groups)

    def kernel(
        x_ref, teach_ref, owner_in, slot_in, b_ref, wup_hbm, wdn_hbm, wad_hbm,
        ga_ref, ig_ref,
        wup, wdn, wad, wsem,
        normed, hidden, dgelu, full, part, send1, recv1, ybuf,
        s1_s, s1_r, y_s, y_r, ag_s, ag_r,
        outgoing, incoming, qt, t_s, t_r,
        adapted, delta, gh, gpre, gtot,
        so_mate, d_mate, gsum, zsend, zrecv, gfull, so_s, so_r, d_s, d_r, gz_s, gz_r, az_s, az_r, ax_s, ax_r,
        oscr, o_s, o_r, owner_ref, slot_ref, out_s,
    ):
        g = lax.axis_index("group")
        t = lax.axis_index("tensor")
        core = lax.rem(t, 2)
        y = lax.div(t, 2)
        mate = t + 1 - 2 * core
        own0 = pl.multiple_of(core * half, 16)
        oth0 = pl.multiple_of((1 - core) * half, 16)
        own = pl.ds(own0, half)
        oth = pl.ds(oth0, half)

        gx = lax.rem(g, 2)
        gz = lax.div(g, 2)
        xmate = (gz * 2 + 1 - gx, t)
        def cols(c):
            return slice(c * 128, (c + 1) * 128)

        lane0 = pl.ds(pl.multiple_of(gx * hw, hw), hw)
        lane1 = pl.ds(pl.multiple_of((1 - gx) * hw, hw), hw)

        barrier = pltpu.get_barrier_semaphore()
        for k in range(1, tensors):
            pl.semaphore_signal(barrier, inc=1, device_id=(g, lax.rem(t + k, tensors)), device_id_type=MESH)
        for k in range(1, groups):
            pl.semaphore_signal(barrier, inc=1, device_id=(lax.rem(g + k, groups), t), device_id_type=MESH)

        loads = [
            pltpu.make_async_copy(src, dst, wsem.at[i])
            for i, (src, dst) in enumerate(((wup_hbm, wup), (wdn_hbm, wdn), (wad_hbm, wad)))
        ]
        for c in loads:
            c.start()

        sends = []

        def remote(src, dst, ss, rs, dev):
            c = pltpu.make_async_remote_copy(
                src_ref=src, dst_ref=dst, send_sem=ss, recv_sem=rs, device_id=dev, device_id_type=MESH
            )
            c.start()
            sends.append(c)
            return c

        xf = x_ref[...].astype(F32)
        cen = jnp.mean(xf, axis=-1, keepdims=True)
        dev_ = xf - cen
        rstd = lax.rsqrt(jnp.mean(jnp.square(dev_), axis=-1, keepdims=True) + 1e-06)
        normed[...] = (dev_ * rstd).astype(BF16)
        for s in range(groups):
            owner_ref[s:s + 1, :] = owner_in[s * tok:(s + 1) * tok][None, :]
            slot_ref[s:s + 1, :] = slot_in[s * tok:(s + 1) * tok][None, :]
        ir = lax.broadcasted_iota(jnp.int32, (tok, tok), 0)
        ic = lax.broadcasted_iota(jnp.int32, (tok, tok), 1)
        own_row = owner_ref[pl.ds(g, 1), :]
        own_bc = jnp.broadcast_to(own_row, (tok, tok))
        own_col = jnp.sum(jnp.where(ir == ic, own_bc, 0).astype(F32), axis=1, keepdims=True)
        before = ir < ic
        same = jnp.where((own_col == own_bc.astype(F32)) & before, 1.0, 0.0)
        rank_row = jnp.sum(same, axis=0, keepdims=True)
        place = own_row.astype(F32) * slots + rank_row
        srow = lax.broadcasted_iota(jnp.int32, (groups * slots, tok), 0).astype(F32)
        pick = jnp.where(srow == place, 1.0, 0.0).astype(BF16)
        outgoing[...] = mm(pick, teach_ref[...]).astype(BF16).reshape(groups, slots, fw)
        pl.semaphore_wait(barrier, tensors - 1 + groups - 1)
        teach = []
        for k in range(1, groups):
            to = lax.rem(g + k, groups)
            teach.append(
                remote(outgoing.at[to], incoming.at[g], t_s.at[k - 1], t_r.at[k - 1], (to, t))
            )
        incoming[g] = outgoing[g]
        loads[0].wait()
        for j in range(ff // uw):
            cs = slice(j * uw, (j + 1) * uw)
            pre = mm(normed[...], wup[:, cs]) + b_ref[cs][None, :]
            sq = pre * pre
            th = jnp.tanh(GELU_K * pre * (1.0 + GELU_A * sq))
            hidden[:, cs] = (0.5 * pre * (1.0 + th)).astype(BF16)
            dgelu[:, cs] = 0.5 * (1.0 + th) + 0.5 * GELU_K * pre * (1.0 - th * th) * (1.0 + 3.0 * GELU_A * sq)

        loads[1].wait()

        state = {}

        def stage1(a, j, value):
            part[a, j] = value
            send1[a, j] = part[a, j, oth, :].astype(BF16)
            state["s1", a, j] = remote(
                send1.at[a, j], recv1.at[a, j], s1_s.at[a, j], s1_r.at[a, j], (g, mate)
            )

        def stage2(a, j):
            state["s1", a, j].wait_recv()
            ybuf[a, j, y] = (part[a, j, own, :] + recv1[a, j].astype(F32)).astype(BF16)
            state["y", a, j] = [
                remote(
                    ybuf.at[a, j, y], ybuf.at[a, j, y], y_s.at[a, j, k - 1], y_r.at[a, j, k - 1],
                    (g, lax.rem(y + k, ny) * 2 + core),
                )
                for k in range(1, ny)
            ]

        def total(a, j):
            for c in state["y", a, j]:
                c.wait_recv()
            s = ybuf[a, j, 0].astype(F32)
            for k in range(1, ny):
                s = s + ybuf[a, j, k].astype(F32)
            return s

        def stage3(a, j, finish):
            full[a, j, own, :] = finish(total(a, j), j).astype(BF16)
            state["ag", a, j] = remote(
                full.at[a, j, own, :], full.at[a, j, own, :], ag_s.at[a, j], ag_r.at[a, j], (g, mate)
            )
            if a == 0 and reduce_groups:
                state["so", j] = remote(
                    full.at[0, j, own, lane1], so_mate.at[j, own, :], so_s.at[0, j], so_r.at[0, j], xmate
                )

        def reduce_loop(a, product):
            for j in range(nc):
                stage1(a, j, product(j))
                if j >= 1:
                    stage2(a, j - 1)
            stage2(a, nc - 1)

        def gather_loop(a, finish, consume):
            for j in range(nc):
                stage3(a, j, finish)
                if j >= 1:
                    state["ag", a, j - 1].wait_recv()
                    consume(j - 1)
            state["ag", a, nc - 1].wait_recv()
            consume(nc - 1)

        reduce_loop(0, lambda j: mm(hidden[...], wdn[:, j * cw:(j + 1) * cw]))

        mine = owner_ref[...] == g
        tri = jnp.where(before, 1.0, 0.0).astype(BF16)
        rank = mm(jnp.where(mine, 1.0, 0.0).astype(BF16), tri)
        rank = jnp.where(mine, rank, -1.0)
        dest1 = slot_ref[...].astype(F32) + 1.0
        krow = lax.broadcasted_iota(jnp.int32, (slots, tok), 0).astype(F32)
        lane = lax.broadcasted_iota(jnp.int32, (slots, tok), 1).astype(F32)
        for s in range(groups):
            hit = jnp.where(krow == rank[s:s + 1, :], dest1[s:s + 1, :], 0.0)
            dest = jnp.sum(hit, axis=1, keepdims=True) - 1.0
            qt[s * slots:(s + 1) * slots, :] = jnp.where(lane == dest, 1.0, 0.0).astype(BF16)

        loads[2].wait()
        adapted[...] = jnp.zeros_like(adapted)

        def add_input(s, j):
            return s + x_ref[own, j * cw:(j + 1) * cw].astype(F32)

        def adapt(j):
            adapted[...] += mm(full[0, j], wad[j * cw:(j + 1) * cw, :])

        gather_loop(0, add_input, adapt)
        for c in teach:
            c.wait_recv()
        target = mm(qt[...], incoming[...].reshape(groups * slots, fw), TN)
        delta[...] = (adapted[...] - target).astype(BF16)

        if reduce_groups:
            dcopy = [
                remote(delta.at[:, cols(c)], d_mate.at[:, cols(c)], d_s.at[c], d_r.at[c], xmate) for c in range(nch)
            ]

        reduce_loop(1, lambda j: mm(delta[...], wad[j * cw:(j + 1) * cw, :], NT))

        zcopy, azcopy, axcopy = {}, {}, {}

        def rows(zz):
            return pl.ds(pl.multiple_of(zz * blk, 16), blk)

        def z_send():
            for j in range(nc):
                state["so", j].wait_recv()
                state["so2", j] = remote(
                    so_mate.at[j, own, :], so_mate.at[j, own, :], so_s.at[1, j], so_r.at[1, j], (g, mate)
                )
            for j in range(nc):
                v = mm(full[0, j, :, lane0], delta[...], TN)
                for c in range(nch):
                    gsum[c, j * hw:(j + 1) * hw, :] = v[:, cols(c)]
            for c in range(nch):
                dcopy[c].wait_recv()
            for j in range(nc):
                state["so2", j].wait_recv()
                v = mm(so_mate[j], d_mate[...], TN)
                for c in range(nch):
                    w = gsum[c, j * hw:(j + 1) * hw, :] + v[:, cols(c)]
                    gsum[c, j * hw:(j + 1) * hw, :] = w
                    zsend[c, j * hw:(j + 1) * hw, :] = w.astype(BF16)
            for c in range(nch):
                for k in range(1, nz):
                    zz = lax.rem(gz + k, nz)
                    zcopy[c, k] = remote(
                        zsend.at[c, rows(zz), :], zrecv.at[c, k - 1], gz_s.at[c, k - 1], gz_r.at[c, k - 1],
                        (zz * 2 + gx, t),
                    )

        def z_sum(c):
            s = gsum[c, rows(gz), :]
            for k in range(1, nz):
                zcopy[c, k].wait_recv()
                s = s + zrecv[c, k - 1].astype(F32)
            gfull[c, gx, rows(gz), :] = (s * scale).astype(BF16)
            blkref = gfull.at[c, gx, rows(gz), :]
            for k in range(1, nz):
                zz = lax.rem(gz + k, nz)
                azcopy[c, k] = remote(blkref, blkref, az_s.at[c, k - 1], az_r.at[c, k - 1], (zz * 2 + gx, t))
            axcopy[c, 0] = remote(blkref, blkref, ax_s.at[c, 0], ax_r.at[c, 0], xmate)

        def z_gather(c):
            for k in range(1, nz):
                azcopy[c, k].wait_recv()
                blkref = gfull.at[c, gx, rows(lax.rem(gz - k + nz, nz)), :]
                axcopy[c, k] = remote(blkref, blkref, ax_s.at[c, k], ax_r.at[c, k], xmate)

        if reduce_groups:
            z_send()
        else:
            for j in range(nc):
                ga_ref[j * cw:(j + 1) * cw, :] = mm(full[0, j], delta[...], TN)

        gh[...] = jnp.zeros_like(gh)

        def back(j):
            gh[...] += mm(full[1, j], wdn[:, j * cw:(j + 1) * cw], NT)

        gather_loop(1, lambda s, j: s, back)
        gpre[...] = (gh[...] * dgelu[...]).astype(BF16)
        if reduce_groups:
            z_sum(0)
        reduce_loop(2, lambda j: mm(gpre[...], wup[j * cw:(j + 1) * cw, :], NT))
        if reduce_groups:
            for c in range(1, nch):
                z_sum(c)
        for j in range(nc):
            gtot[:, j * cw:(j + 1) * cw] = total(2, j)
        gn = gtot[...]
        xo = x_ref[own, :].astype(F32)
        cen = jnp.mean(xo, axis=-1, keepdims=True)
        dv = xo - cen
        r = lax.rsqrt(jnp.mean(jnp.square(dv), axis=-1, keepdims=True) + 1e-06)
        yn = dv * r
        gmean = jnp.mean(gn, axis=-1, keepdims=True)
        gy = jnp.mean(gn * yn, axis=-1, keepdims=True)
        dx = r * (gn - gmean - yn * gy)
        for j in range(nc):
            cs = slice(j * cw, (j + 1) * cw)
            oscr[own, cs] = (full[1, j, own, :].astype(F32) + dx[:, cs]).astype(BF16)
        ocopy = remote(oscr.at[own, :], oscr.at[own, :], o_s.at[0], o_r.at[0], (g, mate))
        if reduce_groups:
            for c in range(nch):
                z_gather(c)
        ocopy.wait_recv()
        outs = [pltpu.make_async_copy(oscr, ig_ref, out_s.at[nch])]
        outs[0].start()
        if reduce_groups:
            for c in range(nch):
                for k in range(nz):
                    axcopy[c, k].wait_recv()
                outs.append(pltpu.make_async_copy(gfull.at[c], ga_ref.at[c], out_s.at[c]))
                outs[-1].start()
        for c in outs:
            c.wait()
        for c in sends:
            c.wait_send()

    vm = pltpu.VMEM
    dma = pltpu.SemaphoreType.DMA
    gb = (nch, d // 2, 128) if reduce_groups else (1, 16, 128)
    zb = (nch, nz - 1, blk, 128) if reduce_groups else (1, 1, 16, 128)
    fb = (nch, 2, d // 2, 128) if reduce_groups else (1, 1, 16, 128)
    mb = (nc, tok, hw) if reduce_groups else (1, 16, 128)
    db = (tok, fw) if reduce_groups else (16, 128)
    nsem = nz if reduce_groups else 1
    scratch = [
        vm((d, ff), BF16), vm((ff, d), BF16), vm((d, fw), BF16), dma((3,)),
        vm((tok, d), BF16), vm((tok, ff), BF16), vm((tok, ff), F32),
        vm((2, nc, tok, cw), BF16), vm((3, nc, tok, cw), F32),
        vm((3, nc, half, cw), BF16), vm((3, nc, half, cw), BF16), vm((3, nc, ny, half, cw), BF16),
        dma((3, nc)), dma((3, nc)), dma((3, nc, ny - 1)), dma((3, nc, ny - 1)), dma((2, nc)), dma((2, nc)),
        vm((groups, slots, fw), BF16), vm((groups, slots, fw), BF16), vm((groups * slots, tok), BF16),
        dma((groups - 1,)), dma((groups - 1,)),
        vm((tok, fw), F32), vm((tok, fw), BF16), vm((tok, ff), F32), vm((tok, ff), BF16), vm((half, d), F32),
        vm(mb, BF16), vm(db, BF16), vm(gb, F32), vm(gb, BF16), vm(zb, BF16), vm(fb, BF16),
        dma((2, nc)), dma((2, nc)), dma((nch,)), dma((nch,)), dma((nch, nsem)), dma((nch, nsem)),
        dma((nch, nsem)), dma((nch, nsem)), dma((nch, nsem)), dma((nch, nsem)),
        vm((tok, d), BF16), dma((1,)), dma((1,)), vm((groups, tok), jnp.int32), vm((groups, tok), jnp.int32),
        dma((nch + 1,)),
    ]
    vspec = pl.BlockSpec(memory_space=pltpu.VMEM)
    aspec = pl.BlockSpec(memory_space=pl.ANY)
    return pl.pallas_call(
        kernel,
        out_shape=(jax.ShapeDtypeStruct(fb if reduce_groups else (d, fw), BF16 if reduce_groups else F32), jax.ShapeDtypeStruct((tok, d), BF16)),
        in_specs=[vspec] * 5 + [aspec] * 3,
        out_specs=(aspec if reduce_groups else vspec, aspec),
        scratch_shapes=scratch,
        compiler_params=pltpu.CompilerParams(
            collective_id=0, has_side_effects=True, vmem_limit_bytes=56 * 1024 * 1024
        ),
    )


def widen(packed, rows, d, fw):
    nch = fw // 128
    nc = d // 256

    def kernel(p_hbm, r_hbm, w_hbm, o_hbm, p, w, r, in_s, out_s):
        ins = [pltpu.make_async_copy(p_hbm.at[c], p.at[c], in_s.at[c]) for c in range(nch)]
        row_in = pltpu.make_async_copy(r_hbm, r, in_s.at[nch])
        row_out = pltpu.make_async_copy(r, o_hbm, out_s.at[nc])
        for c in ins:
            c.start()
        row_in.start()
        for c in ins:
            c.wait()
        row_in.wait()
        row_out.start()
        outs = []
        for j in range(nc):
            for c in range(nch):
                for x in range(2):
                    r0 = j * 256 + x * 128
                    w[r0:r0 + 128, c * 128:(c + 1) * 128] = p[c, x, j * 128:(j + 1) * 128, :].astype(F32)
            part = pl.ds(j * 256, 256)
            outs.append(pltpu.make_async_copy(w.at[part, :], w_hbm.at[part, :], out_s.at[j]))
            outs[-1].start()
        for c in outs:
            c.wait()
        row_out.wait()

    any_ = pl.BlockSpec(memory_space=pl.ANY)
    return pl.pallas_call(
        kernel,
        out_shape=(jax.ShapeDtypeStruct((d, fw), F32), jax.ShapeDtypeStruct(rows.shape, rows.dtype)),
        in_specs=[any_] * 2,
        out_specs=(any_, any_),
        scratch_shapes=[
            pltpu.VMEM(packed.shape, BF16), pltpu.VMEM((d, fw), F32), pltpu.VMEM(rows.shape, BF16),
            pltpu.SemaphoreType.DMA((nch + 1,)), pltpu.SemaphoreType.DMA((nc + 1,)),
        ],
    )(packed, rows)


def solution(mesh):
    groups = mesh.shape["group"]
    tensors = mesh.shape["tensor"]

    def per_device(student_in, teacher_feat, owner, slot_row, w_up, b_up, w_down, w_adapt):
        tok, d = student_in.shape
        fw = teacher_feat.shape[1]
        ff = w_up.shape[1]
        reduce_groups = groups % 2 == 0 and d % (groups * 16) == 0 and fw % 128 == 0
        call = make_kernel(groups, tensors, tok, d, ff, fw, reduce_groups)
        grad_adapt, input_grad = call(
            student_in, teacher_feat, owner, slot_row, b_up, w_up, w_down, w_adapt,
        )
        if reduce_groups:
            grad_adapt, input_grad = widen(grad_adapt, input_grad, d, fw)
        else:
            grad_adapt = lax.psum(grad_adapt, "group") / math.sqrt(tok * groups)
        return grad_adapt, input_grad

    return jax.shard_map(
        per_device,
        mesh=mesh,
        in_specs=(
            P("group", None),
            P("group", "tensor"),
            P(),
            P(),
            P(None, "tensor"),
            P("tensor"),
            P("tensor", None),
            P(None, "tensor"),
        ),
        out_specs=(P(None, "tensor"), P("group", None)),
        check_vma=False,
    )
```
